32 devices in a mesh: grp: 2 (over y), gx: 4 (over z), gy: 2 (over x), wa: 2 (over core).
Axes of the slice: x: 2, y: 2, z: 4, core: 2. Of those that a mesh axis runs over, the one named last changes fastest.
Arguments:
- fine_iterate: float32 [128, 128, 1024], P(('grp', 'gx'), 'gy', 'wa'), parts along dimension 0, may hold values from -6 to 6
- fine_rhs: float32 [128, 128, 1024], P(('grp', 'gx'), 'gy', 'wa'), parts along dimension 0, may hold values from -6 to 6
- fine_ids: int32 [128, 128, 1024], P(('grp', 'gx'), 'gy', 'wa'), parts along dimension 0, may hold values from 0 to 7
- level_iterate: float32 [64, 64, 512], P(('grp', 'gx')), parts along dimension 0, may hold values from -6 to 6
- level_rhs: float32 [64, 64, 512], P(('grp', 'gx')), parts along dimension 0, may hold values from -6 to 6
- level_ids: int32 [64, 64, 512], P(('grp', 'gx')), parts along dimension 0, may hold values from 0 to 7
- coarse_update: float32 [32, 32, 256], P(('grp', 'gx')), parts along dimension 0, may hold values from -6 to 6
- conductivity: float32 [8], replicated, may hold values from 0.1 to 10
Outputs:
- smoothed: float32 [128, 128, 1024], P(('grp', 'gx'), 'gy', 'wa'), parts along dimension 0
The draws below stay inside these ranges and needn't reach their ends.
There are 2 independent parts, one for each index of `grp`. The reference program is written for one: setup_inputs(seed, part) draws one part's arguments, and reference() takes and returns one part's arrays. A program takes and returns all parts, laid end to end along the dimension named above; an argument that names none is the same for every part. Nothing has to cross between parts.
All inputs are finite; a program needn't handle non-finite values.
Results may differ from the reference program's by a relative error of at most 0.00012.
Values sent between devices are 32-bit elements; how exact they have to be, the bound alone decides.
A program may use at most 128 MiB of HBM per device.

```python
import math
import jax
import jax.numpy as jnp
from jax import lax

MATERIALS = 8
NZ = 64
NY = 128
NX = 1024


def set_ends(entries, key, least, high):
    longest = entries.shape.index(max(entries.shape))
    spots = []
    for shift in (0, 1):
        where = [jax.random.randint(jax.random.fold_in(key, axis), (), 0, length) for axis, length in enumerate(entries.shape)]
        where[longest] = (where[longest] + shift) % entries.shape[longest]
        spots.append(tuple(where))
    return entries.at[spots[0]].set(least).at[spots[1]].set(high)


def shard_levels(own_key, extent, cuts, low, high):
    loudness, own = 1.0, jax.random.fold_in(own_key, 6)
    for position, shards_of in cuts:
        draws = jnp.exp(jax.random.uniform(jax.random.fold_in(own, position), (shards_of,), jnp.float32, low / len(cuts), high / len(cuts)))
        loudness = loudness * jnp.repeat(draws, extent[position] // shards_of).reshape([-1 if axis == position else 1 for axis in range(len(extent))])
    return loudness


def scatter_about(rng, shape, width, bound, split=(), kind=jnp.bfloat16):
    values = width * jax.random.normal(rng, shape, jnp.float32)
    if split:
        values = values * shard_levels(rng, shape, split, -0.22, 0.18)
    return jnp.clip(values, -bound, bound).astype(kind)


def setup_inputs(seed: int = 0, part: int = 0) -> dict:
    key_list = jax.random.split(jax.random.key(seed), 9)
    part_keys = jax.random.split(jax.random.fold_in(key_list[8], part), 9)
    fine_iterate = scatter_about(part_keys[0], (NZ, NY, NX), 1.0, 6.0, ((0, 4), (1, 2), (2, 2)), jnp.float32)
    fine_rhs = scatter_about(part_keys[1], (NZ, NY, NX), 1.0, 6.0, ((0, 4), (1, 2), (2, 2)), jnp.float32)
    fine_ids = set_ends(jax.random.randint(part_keys[2], (NZ, NY, NX), 0, MATERIALS), jax.random.fold_in(part_keys[2], 1), 0, MATERIALS - 1).astype(jnp.int32)
    level_iterate = scatter_about(part_keys[3], (NZ // 2, NY // 2, NX // 2), 1.0, 6.0, ((0, 4),), jnp.float32)
    level_rhs = scatter_about(part_keys[4], (NZ // 2, NY // 2, NX // 2), 1.0, 6.0, ((0, 4),), jnp.float32)
    level_ids = set_ends(jax.random.randint(part_keys[5], (NZ // 2, NY // 2, NX // 2), 0, MATERIALS), jax.random.fold_in(part_keys[5], 1), 0, MATERIALS - 1).astype(jnp.int32)
    coarse_update = scatter_about(part_keys[6], (NZ // 4, NY // 4, NX // 4), 1.0, 6.0, ((0, 4),), jnp.float32)
    conductivity = jnp.clip(jnp.exp(jax.random.uniform(key_list[7], (MATERIALS,), jnp.float32, math.log(0.1), math.log(10.0))), 0.1, 10.0)
    return {"fine_iterate": fine_iterate, "fine_rhs": fine_rhs, "fine_ids": fine_ids, "level_iterate": level_iterate, "level_rhs": level_rhs, "level_ids": level_ids, "coarse_update": coarse_update, "conductivity": conductivity}


def lookup(ids, table):
    kappa = jnp.zeros(ids.shape, jnp.float32)
    for material in range(MATERIALS):
        kappa = jnp.where(ids == material, table[material], kappa)
    return kappa


def pad_all(field):
    return jnp.pad(field, 1)


def neighbours(ext):
    return [ext[:-2, 1:-1, 1:-1], ext[2:, 1:-1, 1:-1], ext[1:-1, :-2, 1:-1],
            ext[1:-1, 2:, 1:-1], ext[1:-1, 1:-1, :-2], ext[1:-1, 1:-1, 2:]]


def face_weights(kappa_ext):
    centre = kappa_ext[1:-1, 1:-1, 1:-1]
    weights = [0.5 * (centre + other) for other in neighbours(kappa_ext)]
    total = weights[0]
    for extra in weights[1:]:
        total = total + extra
    return weights, total


def scaled_residual(field_ext, rhs, weights, total):
    image = total * field_ext[1:-1, 1:-1, 1:-1]
    for weight, other in zip(weights, neighbours(field_ext)):
        image = image - weight * other
    return (rhs - image) / total


def spread_matrix(coarse_len, rim):
    fine_len = 2 * (coarse_len - 2) + 2 * rim
    cols = jnp.arange(fine_len, dtype=jnp.int32) - rim
    base = cols // 2
    parity = cols - 2 * base
    rowsix = jnp.arange(coarse_len, dtype=jnp.int32)[:, None]
    main = (rowsix == base[None, :] + 1).astype(jnp.float32)
    side = (rowsix == base[None, :] + 2 * parity[None, :]).astype(jnp.float32)
    return 0.75 * main + 0.25 * side


def prolong_axis(coarse, axis, rim):
    count = coarse.shape[axis] - 2
    lower = lax.slice_in_dim(coarse, 0, count, axis=axis)
    middle = lax.slice_in_dim(coarse, 1, count + 1, axis=axis)
    upper = lax.slice_in_dim(coarse, 2, count + 2, axis=axis)
    even = 0.75 * middle + 0.25 * lower
    odd = 0.75 * middle + 0.25 * upper
    shape = list(coarse.shape)
    shape[axis] = 2 * count
    fine = jnp.stack([even, odd], axis=axis + 1).reshape(shape)
    if rim:
        first = 0.75 * lax.slice_in_dim(coarse, 0, 1, axis=axis) + 0.25 * lax.slice_in_dim(coarse, 1, 2, axis=axis)
        last = 0.75 * lax.slice_in_dim(coarse, count + 1, count + 2, axis=axis) + 0.25 * lax.slice_in_dim(coarse, count, count + 1, axis=axis)
        fine = jnp.concatenate([first, fine, last], axis=axis)
    return fine


def prolong(coarse, rim):
    field = prolong_axis(coarse, 0, rim)
    field = prolong_axis(field, 1, rim)
    matrix = spread_matrix(field.shape[2], rim)
    flat = field.reshape(-1, field.shape[2])
    out = jnp.dot(flat, matrix, precision=lax.Precision.HIGHEST, preferred_element_type=jnp.float32)
    return out.reshape(field.shape[0], field.shape[1], matrix.shape[1])


def smooth(field, rhs, kappa):
    weights, total = face_weights(pad_all(kappa))
    step_one = scaled_residual(pad_all(field), rhs, weights, total) / 1.2
    field = field + step_one
    step_two = (2.0 / 7.0) * step_one + (15.0 / 14.0) * scaled_residual(pad_all(field), rhs, weights, total)
    return field + step_two


def reference(fine_iterate, fine_rhs, fine_ids, level_iterate, level_rhs, level_ids, coarse_update, conductivity):
    start = level_iterate + prolong(pad_all(coarse_update), 0)
    middle = smooth(start, level_rhs, lookup(level_ids, conductivity))
    begun = fine_iterate + prolong(pad_all(middle), 0)
    return smooth(begun, fine_rhs, lookup(fine_ids, conductivity))
```

```python
import functools

import jax
import jax.numpy as jnp
from jax import lax
from jax.experimental import pallas as pl
from jax.experimental.pallas import tpu as pltpu
from jax.sharding import PartitionSpec as P

F32 = jnp.float32
HI = lax.Precision.HIGHEST


def lookup(ids, table):
    kappa = jnp.zeros(ids.shape, F32)
    for material, value in enumerate(table):
        kappa = jnp.where(ids == material, value, kappa)
    return kappa


def weights_of(shape, fine_axis, first, total, offset, wrap=None):
    fine = lax.broadcasted_iota(jnp.int32, shape, fine_axis)
    if wrap is not None:
        fine = jnp.where(fine >= wrap[0], fine - wrap[1], fine)
    fine = fine + first
    base = fine >> 1
    side = base + 2 * (fine & 1) - 1
    coarse = lax.broadcasted_iota(jnp.int32, shape, 1 - fine_axis) + offset
    main = jnp.where(coarse == base, 0.75, 0.0)
    both = jnp.where(coarse == side, 0.25, main)
    return jnp.where((fine >= 0) & (fine < total), both, 0.0).astype(F32)


def inverse(kappa, around):
    return jnp.where(kappa > 0.0, 1.0 / (6.0 * kappa + around), 0.0)


def kernel(
    sizes,
    fi_hbm, fr_hbm, fid_hbm, li_hbm, lr_hbm, lid_hbm, co_hbm, table_ref,
    out_ref,
    fi, fr, fid, fiz, fidz, fix, fidx, ysend, yidsend, yrecv, yidrecv,
    li, lr, lid, co, xc,
    lk, lv, lkv, lv1, lkv1, linv, mid, pm,
    fk, fv, fkv, fv1, fkv1, finv, vx, vysend, vyrecv,
    local_sem, send_sem, recv_sem,
):
    count_z, count_y, wr, wc = sizes
    depth, rows, cols = fi.shape
    ldepth, lrows, lcols = li_hbm.shape
    crows, ccols = co_hbm.shape[1:]
    gx = lax.axis_index("gx")
    gy = lax.axis_index("gy")
    wa = lax.axis_index("wa")
    has_zm, has_zp = gx > 0, gx < count_z - 1
    has_ym, has_yp = gy > 0, gy < count_y - 1
    row0 = pl.multiple_of(jnp.clip(gy * (rows // 2) - 8, 0, lrows - wr), 8)
    col0 = pl.multiple_of(wa * (lcols - wc), 128)
    zm, zp = {"gx": gx - 1}, {"gx": gx + 1}
    ym, yp = {"gy": gy - 1}, {"gy": gy + 1}
    other = {"wa": 1 - wa}

    barrier = pltpu.get_barrier_semaphore()
    sides = ((has_zm, zm), (has_zp, zp), (has_ym, ym), (has_yp, yp))
    for there, who in sides:
        @pl.when(there)
        def _(who=who):
            pl.semaphore_signal(barrier, 1, device_id=who, device_id_type=pl.DeviceIdType.MESH)
    pl.semaphore_signal(barrier, 1, device_id=other, device_id_type=pl.DeviceIdType.MESH)

    local = []
    for src, dst in (
        (co_hbm, co.at[pl.ds(2, ldepth // 2)]),
        (li_hbm.at[:, pl.ds(row0, wr), pl.ds(col0, wc)], li.at[pl.ds(3, ldepth)]),
        (lid_hbm.at[:, pl.ds(row0, wr), pl.ds(col0, wc)], lid.at[pl.ds(3, ldepth)]),
        (lr_hbm.at[:, pl.ds(row0, wr), pl.ds(col0, wc)], lr.at[pl.ds(2, ldepth)]),
        (fi_hbm, fi), (fid_hbm, fid), (fr_hbm, fr),
    ):
        copy = pltpu.make_async_copy(src, dst, local_sem.at[len(local)])
        copy.start()
        local.append(copy)

    present = [jnp.where(there, 1, 0) for there, _ in sides]
    pl.semaphore_wait(barrier, present[0] + present[1] + present[2] + present[3] + 1)

    used = [0]

    def send(src, dst, who, to_there, from_there):
        index = used[0]
        used[0] += 1
        copy = pltpu.make_async_remote_copy(
            src_ref=src, dst_ref=dst, send_sem=send_sem.at[index], recv_sem=recv_sem.at[index],
            device_id=who, device_id_type=pl.DeviceIdType.MESH,
        )
        if to_there is None:
            copy.start()
        else:
            pl.when(to_there)(copy.start)
        return copy, to_there, from_there

    def receive(copies):
        for copy, _, there in copies:
            if there is None:
                copy.wait_recv()
            else:
                pl.when(there)(copy.wait_recv)

    def sent(copies):
        for copy, there, _ in copies:
            if there is None:
                copy.wait_send()
            else:
                pl.when(there)(copy.wait_send)

    def z_pair(src, dst, width, own):
        count = src.shape[0]
        win = (pl.ds(row0, wr), pl.ds(col0, wc)) if dst.shape[1] == wr else (slice(None), slice(None))
        return [
            send(src.at[(pl.ds(count - width, width),) + win], dst.at[pl.ds(own - width, width)], zp, has_zp, has_zm),
            send(src.at[(pl.ds(0, width),) + win], dst.at[pl.ds(own + count, width)], zm, has_zm, has_zp),
        ]

    level_in = z_pair(co_hbm, co, 2, 2)
    level_in += z_pair(li_hbm, li, 3, 3)
    level_in += z_pair(lid_hbm, lid, 3, 3)
    level_in += z_pair(lr_hbm, lr, 2, 2)
    edge0 = pl.multiple_of((1 - wa) * (cols - 128), 128)
    fine_in = [
        send(fid_hbm.at[:, :, pl.ds(edge0, 128)], fidx, other, None, None),
        send(fi_hbm.at[:, :, pl.ds(edge0, 128)], fix, other, None, None),
    ]
    for src, dst in ((fid_hbm, fidz), (fi_hbm, fiz)):
        fine_in.append(send(src.at[pl.ds(depth - 1, 1)], dst.at[pl.ds(0, 1)], zp, has_zp, has_zm))
        fine_in.append(send(src.at[pl.ds(0, 1)], dst.at[pl.ds(1, 1)], zm, has_zm, has_zp))
    local[4].wait()
    local[5].wait()
    for src, pack, dst in ((fid, yidsend, yidrecv), (fi, ysend, yrecv)):
        for z in range(depth):
            pack[0, pl.ds(z, 1), :] = src[z, pl.ds(rows - 1, 1), :]
            pack[1, pl.ds(z, 1), :] = src[z, pl.ds(0, 1), :]
        fine_in.append(send(pack.at[0], dst.at[0], yp, has_yp, has_ym))
        fine_in.append(send(pack.at[1], dst.at[1], ym, has_ym, has_yp))

    table = [table_ref[m] for m in range(table_ref.shape[0])]
    mx = weights_of((ccols, wc), 1, col0, lcols, 0)
    my = weights_of((wr, crows), 0, row0, lrows, 0)
    mx2 = weights_of((wc, cols + 128), 1, wa * cols, 2 * lcols, col0, (cols + 64, cols + 128))
    my2 = weights_of((rows + 16, wr), 0, gy * rows - 8, 2 * lrows, row0)

    for copy in local[:4]:
        copy.wait()
    receive(level_in)

    planes = ldepth + 6
    for p in range(ldepth // 2 + 4):
        field = co[p]
        if p < 2:
            field = jnp.where(has_zm, field, 0.0)
        if p >= ldepth // 2 + 2:
            field = jnp.where(has_zp, field, 0.0)
        xc[p] = jnp.dot(field, mx, precision=HI, preferred_element_type=F32)
    lrow = lax.broadcasted_iota(jnp.int32, (wr, wc), 0)
    lcol = lax.broadcasted_iota(jnp.int32, (wr, wc), 1)
    inside = (lrow != jnp.where(gy == 0, wr - 1, 0)) & (lcol != jnp.where(wa == 0, wc - 1, 0))

    def level_start(p, carry):
        base = (p + 1) // 2
        side = base + 2 * ((p + 1) % 2) - 1
        spread = jnp.dot(my, 0.75 * xc[base] + 0.25 * xc[side], precision=HI, preferred_element_type=F32)
        here = ((p >= 3) | has_zm) & ((p < ldepth + 3) | has_zp)
        keep = inside & here
        kappa = jnp.where(keep, lookup(lid[p], table), 0.0)
        field = jnp.where(keep, li[p] + spread, 0.0)
        lk[p] = kappa
        lv[p] = field
        lkv[p] = kappa * field
        return carry

    lax.fori_loop(0, planes, level_start, 0)

    def level_sum(ref, p):
        field = ref[p]
        return (
            pltpu.roll(field, 1, 0) + pltpu.roll(field, wr - 1, 0)
            + pltpu.roll(field, 1, 1) + pltpu.roll(field, wc - 1, 1)
            + ref[p - 1] + ref[p + 1]
        )

    def level_one(p, carry):
        kappa = lk[p]
        inv = inverse(kappa, level_sum(lk, p))
        linv[p] = inv
        rhs = jnp.where(inv > 0.0, lr[p - 1], 0.0)
        goal = (2.0 * rhs + kappa * level_sum(lv, p) + level_sum(lkv, p)) * inv
        field = lv[p]
        new = field + (goal - field) * (1.0 / 1.2)
        lv1[p] = new
        lkv1[p] = kappa * new
        return carry

    lax.fori_loop(1, planes - 1, level_one, 0)

    def level_two(p, carry):
        inv = linv[p]
        rhs = jnp.where(inv > 0.0, lr[p - 1], 0.0)
        goal = (2.0 * rhs + lk[p] * level_sum(lv1, p) + level_sum(lkv1, p)) * inv
        settled = (3.0 / 14.0) * lv1[p] - (2.0 / 7.0) * lv[p] + (15.0 / 14.0) * goal
        mid[...] = jnp.dot(settled, mx2, precision=HI, preferred_element_type=F32)
        pm[p - 2] = jnp.dot(my2, mid[...], precision=HI, preferred_element_type=F32)
        return carry

    lax.fori_loop(2, planes - 2, level_two, 0)

    local[6].wait()
    receive(fine_in)
    lanes = lax.broadcasted_iota(jnp.int32, (16, 128), 1)
    edge_in = jnp.where(wa == 0, 0, 64)
    edge_in = (lanes >= edge_in) & (lanes < edge_in + 64)

    def spread_at(j, where, width):
        base = (j + 1) // 2
        side = base + 2 * ((j + 1) % 2) - 1
        return 0.75 * pm[(base,) + where + (width,)] + 0.25 * pm[(side,) + where + (width,)]

    main = slice(0, cols)
    rim = slice(cols, cols + 128)

    def put(j, where, width, kappa, field):
        fk[(j,) + where + (width,)] = kappa
        fv[(j,) + where + (width,)] = field
        fkv[(j,) + where + (width,)] = kappa * field

    for n, j, there in ((0, 0, has_zm), (1, depth + 1, has_zp)):
        for r in range(0, rows, 16):
            at = (pl.ds(8 + r, 16),)
            put(
                j, at, main,
                jnp.where(there, lookup(fidz[n, r:r + 16, :], table), 0.0),
                jnp.where(there, fiz[n, r:r + 16, :] + spread_at(j, at, main), 0.0),
            )

    def fine_start(j, carry):
        for r in range(0, rows, 16):
            at = (pl.ds(8 + r, 16),)
            put(
                j, at, main,
                lookup(fid[j - 1, r:r + 16, :], table),
                fi[j - 1, r:r + 16, :] + spread_at(j, at, main),
            )
            put(
                j, at, rim,
                jnp.where(edge_in, lookup(fidx[j - 1, r:r + 16, :], table), 0.0),
                jnp.where(edge_in, fix[j - 1, r:r + 16, :] + spread_at(j, at, rim), 0.0),
            )
        for n, row, there in ((0, 7, has_ym), (1, rows + 8, has_yp)):
            at = (pl.ds(row, 1),)
            put(
                j, at, main,
                jnp.where(there, lookup(yidrecv[n, pl.ds(j - 1, 1), :], table), 0.0),
                jnp.where(there, yrecv[n, pl.ds(j - 1, 1), :] + spread_at(j, at, main), 0.0),
            )
        return carry

    lax.fori_loop(1, depth + 1, fine_start, 0)

    def fine_sum(ref, j, r):
        centre = ref[j, r:r + 16, :]
        return (
            pltpu.roll(centre, 1, 1)[:, :cols] + pltpu.roll(centre, cols + 127, 1)[:, :cols]
            + ref[j, r - 1:r + 15, main] + ref[j, r + 1:r + 17, main]
            + ref[j - 1, r:r + 16, main] + ref[j + 1, r:r + 16, main]
        )

    def fine_one(j, carry):
        for r in range(0, rows, 16):
            s = 8 + r
            kappa = fk[j, s:s + 16, main]
            inv = 1.0 / (6.0 * kappa + fine_sum(fk, j, s))
            finv[j - 1, r:r + 16, :] = inv
            goal = (2.0 * fr[j - 1, r:r + 16, :] + kappa * fine_sum(fv, j, s) + fine_sum(fkv, j, s)) * inv
            field = fv[j, s:s + 16, main]
            new = field + (goal - field) * (1.0 / 1.2)
            fv1[j, s:s + 16, main] = new
            fkv1[j, s:s + 16, main] = kappa * new
        return carry

    lax.fori_loop(1, depth + 1, fine_one, 0)

    own = pl.ds(8, rows)
    fine_out = [
        send(fv1.at[pl.ds(depth, 1), own, pl.ds(0, cols)], fv1.at[pl.ds(0, 1), own, pl.ds(0, cols)], zp, has_zp, has_zm),
        send(fv1.at[pl.ds(1, 1), own, pl.ds(0, cols)], fv1.at[pl.ds(depth + 1, 1), own, pl.ds(0, cols)], zm, has_zm, has_zp),
        send(fv1.at[pl.ds(1, depth), own, pl.ds(edge0, 128)], vx, other, None, None),
    ]
    for z in range(depth):
        vysend[0, pl.ds(z, 1), :] = fv1[z + 1, pl.ds(rows + 7, 1), main]
        vysend[1, pl.ds(z, 1), :] = fv1[z + 1, pl.ds(8, 1), main]
    fine_out.append(send(vysend.at[0], vyrecv.at[0], yp, has_yp, has_ym))
    fine_out.append(send(vysend.at[1], vyrecv.at[1], ym, has_ym, has_yp))
    receive(fine_out)

    for j, there in ((0, has_zm), (depth + 1, has_zp)):
        for r in range(8, rows + 8, 16):
            field = jnp.where(there, fv1[j, r:r + 16, main], 0.0)
            fv1[j, r:r + 16, main] = field
            fkv1[j, r:r + 16, main] = fk[j, r:r + 16, main] * field

    def fine_rims(j, carry):
        for r in range(0, rows, 16):
            s = 8 + r
            field = jnp.where(edge_in, vx[j - 1, r:r + 16, :], 0.0)
            fv1[j, s:s + 16, rim] = field
            fkv1[j, s:s + 16, rim] = fk[j, s:s + 16, rim] * field
        for n, row, there in ((0, 7, has_ym), (1, rows + 8, has_yp)):
            field = jnp.where(there, vyrecv[n, pl.ds(j - 1, 1), :], 0.0)
            fv1[j, pl.ds(row, 1), main] = field
            fkv1[j, pl.ds(row, 1), main] = fk[j, pl.ds(row, 1), main] * field
        return carry

    lax.fori_loop(1, depth + 1, fine_rims, 0)

    def fine_two(j, carry):
        for r in range(0, rows, 16):
            s = 8 + r
            goal = (
                2.0 * fr[j - 1, r:r + 16, :] + fk[j, s:s + 16, main] * fine_sum(fv1, j, s) + fine_sum(fkv1, j, s)
            ) * finv[j - 1, r:r + 16, :]
            out_ref[j - 1, r:r + 16, :] = (
                (3.0 / 14.0) * fv1[j, s:s + 16, main] - (2.0 / 7.0) * fv[j, s:s + 16, main] + (15.0 / 14.0) * goal
            )
        return carry

    sent(level_in + fine_in + fine_out)
    lax.fori_loop(1, depth + 1, fine_two, 0)


def per_device(sizes, *args):
    fine, level, coarse = args[0], args[3], args[6]
    count_z, count_y, wr, wc = sizes
    depth, rows, cols = fine.shape
    ldepth = level.shape[0]
    i32 = jnp.int32
    planes = ldepth + 6
    big = (depth + 2, rows + 16, cols + 128)
    small = (planes, wr, wc)

    def vmem(shape, dtype=F32):
        return pltpu.VMEM(shape, dtype)

    scratch = [
        vmem(fine.shape), vmem(fine.shape), vmem(fine.shape, i32),
        vmem((2, rows, cols)), vmem((2, rows, cols), i32),
        vmem((depth, rows, 128)), vmem((depth, rows, 128), i32),
        vmem((2, depth, cols)), vmem((2, depth, cols), i32),
        vmem((2, depth, cols)), vmem((2, depth, cols), i32),
        vmem(small), vmem((ldepth + 4, wr, wc)), vmem(small, i32),
        vmem((ldepth // 2 + 4,) + coarse.shape[1:]),
        vmem((ldepth // 2 + 4, coarse.shape[1], wc)),
        vmem(small), vmem(small), vmem(small), vmem(small), vmem(small), vmem(small),
        vmem((wr, cols + 128)), vmem((ldepth + 2, rows + 16, cols + 128)),
        vmem(big), vmem(big), vmem(big), vmem(big), vmem(big), vmem(fine.shape),
        vmem((depth, rows, 128)), vmem((2, depth, cols)), vmem((2, depth, cols)),
        pltpu.SemaphoreType.DMA((7,)),
        pltpu.SemaphoreType.DMA((23,)),
        pltpu.SemaphoreType.DMA((23,)),
    ]
    return pl.pallas_call(
        functools.partial(kernel, sizes),
        out_shape=jax.ShapeDtypeStruct(fine.shape, F32),
        in_specs=[pl.BlockSpec(memory_space=pl.ANY)] * 7 + [pl.BlockSpec(memory_space=pltpu.SMEM)],
        out_specs=pl.BlockSpec(memory_space=pltpu.VMEM),
        scratch_shapes=scratch,
        compiler_params=pltpu.CompilerParams(
            collective_id=0, has_side_effects=True, vmem_limit_bytes=56 * 1024 * 1024
        ),
    )(*args)


def solution(mesh):
    count_z, count_y = mesh.shape["gx"], mesh.shape["gy"]
    sizes = (count_z, count_y, 40 if count_y <= 2 else 48, 384)
    return jax.shard_map(
        functools.partial(per_device, sizes),
        mesh=mesh,
        in_specs=(
            P(("grp", "gx"), "gy", "wa"),
            P(("grp", "gx"), "gy", "wa"),
            P(("grp", "gx"), "gy", "wa"),
            P(("grp", "gx"), None, None),
            P(("grp", "gx"), None, None),
            P(("grp", "gx"), None, None),
            P(("grp", "gx"), None, None),
            P(),
        ),
        out_specs=P(("grp", "gx"), "gy", "wa"),
        check_vma=False,
    )
```

```python
import functools

import jax
import jax.numpy as jnp
from jax import lax
from jax.experimental import pallas as pl
from jax.experimental.pallas import tpu as pltpu
from jax.sharding import PartitionSpec as P

F32 = jnp.float32
BF16 = jnp.bfloat16


def lookup(ids, table):
    kappa = jnp.zeros(ids.shape, F32)
    for material, value in enumerate(table):
        kappa = jnp.where(ids == material, value, kappa)
    return kappa


def weights_of(shape, fine_axis, first, total, offset, wrap=None):
    fine = lax.broadcasted_iota(jnp.int32, shape, fine_axis)
    if wrap is not None:
        fine = jnp.where(fine >= wrap[0], fine - wrap[1], fine)
    fine = fine + first
    base = fine >> 1
    side = base + 2 * (fine & 1) - 1
    coarse = lax.broadcasted_iota(jnp.int32, shape, 1 - fine_axis) + offset
    main = jnp.where(coarse == base, 0.75, 0.0)
    both = jnp.where(coarse == side, 0.25, main)
    return jnp.where((fine >= 0) & (fine < total), both, 0.0).astype(F32)


def halves(field, axis):
    high = field.astype(BF16).astype(F32)
    return jnp.concatenate([high, field - high], axis=axis).astype(BF16)


def twice(weights, axis):
    return jnp.concatenate([weights, weights], axis=axis).astype(BF16)


def inverse(kappa, around):
    return jnp.where(kappa > 0.0, 1.0 / (6.0 * kappa + around), 0.0)


def kernel(
    sizes,
    fi_hbm, fr_hbm, fid_hbm, li_hbm, lr_hbm, lid_hbm, co_hbm, table_ref,
    out_ref,
    fi, fr, fid, fiz, fidz, fix, fidx, ysend, yidsend, yrecv, yidrecv,
    li, lr, lid, co, xc,
    lk, lv, lkv, lv1, lkv1, linv, mid, wide, pm,
    fk, fv, fkv, fv1, fkv1, finv, vx, vysend, vyrecv,
    local_sem, send_sem, recv_sem,
):
    count_z, count_y, wr, wc = sizes
    depth, rows, cols = fi.shape
    ldepth, lrows, lcols = li_hbm.shape
    crows, ccols = co_hbm.shape[1:]
    gx = lax.axis_index("gx")
    gy = lax.axis_index("gy")
    wa = lax.axis_index("wa")
    has_zm, has_zp = gx > 0, gx < count_z - 1
    has_ym, has_yp = gy > 0, gy < count_y - 1
    row0 = pl.multiple_of(jnp.clip(gy * (rows // 2) - 8, 0, lrows - wr), 8)
    col0 = pl.multiple_of(wa * (lcols - wc), 128)
    zm, zp = {"gx": gx - 1}, {"gx": gx + 1}
    ym, yp = {"gy": gy - 1}, {"gy": gy + 1}
    other = {"wa": 1 - wa}

    barrier = pltpu.get_barrier_semaphore()
    sides = ((has_zm, zm), (has_zp, zp), (has_ym, ym), (has_yp, yp))
    for there, who in sides:
        @pl.when(there)
        def _(who=who):
            pl.semaphore_signal(barrier, 1, device_id=who, device_id_type=pl.DeviceIdType.MESH)
    pl.semaphore_signal(barrier, 1, device_id=other, device_id_type=pl.DeviceIdType.MESH)

    local = []
    for src, dst in (
        (co_hbm, co.at[pl.ds(2, ldepth // 2)]),
        (li_hbm.at[:, pl.ds(row0, wr), pl.ds(col0, wc)], li.at[pl.ds(3, ldepth)]),
        (lid_hbm.at[:, pl.ds(row0, wr), pl.ds(col0, wc)], lid.at[pl.ds(3, ldepth)]),
        (lr_hbm.at[:, pl.ds(row0, wr), pl.ds(col0, wc)], lr.at[pl.ds(2, ldepth)]),
        (fi_hbm, fi), (fid_hbm, fid), (fr_hbm, fr),
    ):
        copy = pltpu.make_async_copy(src, dst, local_sem.at[len(local)])
        copy.start()
        local.append(copy)

    present = [jnp.where(there, 1, 0) for there, _ in sides]
    pl.semaphore_wait(barrier, present[0] + present[1] + present[2] + present[3] + 1)

    used = [0]

    def send(src, dst, who, to_there, from_there):
        index = used[0]
        used[0] += 1
        copy = pltpu.make_async_remote_copy(
            src_ref=src, dst_ref=dst, send_sem=send_sem.at[index], recv_sem=recv_sem.at[index],
            device_id=who, device_id_type=pl.DeviceIdType.MESH,
        )
        if to_there is None:
            copy.start()
        else:
            pl.when(to_there)(copy.start)
        return copy, to_there, from_there

    def receive(copies):
        for copy, _, there in copies:
            if there is None:
                copy.wait_recv()
            else:
                pl.when(there)(copy.wait_recv)

    def sent(copies):
        for copy, there, _ in copies:
            if there is None:
                copy.wait_send()
            else:
                pl.when(there)(copy.wait_send)

    def z_pair(src, dst, width, own):
        count = src.shape[0]
        win = (pl.ds(row0, wr), pl.ds(col0, wc)) if dst.shape[1] == wr else (slice(None), slice(None))
        return [
            send(src.at[(pl.ds(count - width, width),) + win], dst.at[pl.ds(own - width, width)], zp, has_zp, has_zm),
            send(src.at[(pl.ds(0, width),) + win], dst.at[pl.ds(own + count, width)], zm, has_zm, has_zp),
        ]

    coarse_in = z_pair(co_hbm, co, 2, 2)
    level_in = z_pair(li_hbm, li, 3, 3)
    level_in += z_pair(lid_hbm, lid, 3, 3)
    level_in += z_pair(lr_hbm, lr, 2, 2)
    edge0 = pl.multiple_of((1 - wa) * (cols - 128), 128)
    fine_in = [
        send(fid_hbm.at[:, :, pl.ds(edge0, 128)], fidx, other, None, None),
        send(fi_hbm.at[:, :, pl.ds(edge0, 128)], fix, other, None, None),
    ]
    local[4].wait()
    local[5].wait()
    for src, pack, dst in ((fid, yidsend, yidrecv), (fi, ysend, yrecv)):
        for z in range(depth):
            pack[0, pl.ds(z, 1), :] = src[z, pl.ds(rows - 1, 1), :]
            pack[1, pl.ds(z, 1), :] = src[z, pl.ds(0, 1), :]
        fine_in.append(send(pack.at[0], dst.at[0], yp, has_yp, has_ym))
        fine_in.append(send(pack.at[1], dst.at[1], ym, has_ym, has_yp))

    table = [table_ref[m] for m in range(table_ref.shape[0])]
    main = slice(0, cols)
    rim = slice(cols, cols + 128)

    def fine_kappa(j, carry):
        for r in range(0, rows, 16):
            fk[j, 8 + r:24 + r, main] = lookup(fid[j - 1, r:r + 16, :], table)
        return carry

    lax.fori_loop(1, depth + 1, fine_kappa, 0)

    mx = twice(weights_of((ccols, wc), 1, col0, lcols, 0), 0)
    my = twice(weights_of((wr, crows), 0, row0, lrows, 0), 1)
    mx2 = twice(weights_of((wc, cols + 128), 1, wa * cols, 2 * lcols, col0, (cols + 64, cols + 128)), 0)
    my2 = twice(weights_of((rows + 16, wr), 0, gy * rows - 8, 2 * lrows, row0), 1)

    for copy in local[:4]:
        copy.wait()
    receive(coarse_in)

    planes = ldepth + 6
    cplanes = ldepth // 2 + 4
    coarse = jnp.concatenate(
        [jnp.where(has_zm, co[0:2], 0.0), co[2:cplanes - 2], jnp.where(has_zp, co[cplanes - 2:], 0.0)], axis=0
    )
    xc[...] = jnp.dot(
        halves(coarse.reshape(cplanes * crows, ccols), 1), mx, preferred_element_type=F32
    ).reshape(cplanes, crows, wc)
    lrow = lax.broadcasted_iota(jnp.int32, (wr, wc), 0)
    lcol = lax.broadcasted_iota(jnp.int32, (wr, wc), 1)
    inside = (lrow != jnp.where(gy == 0, wr - 1, 0)) & (lcol != jnp.where(wa == 0, wc - 1, 0))

    def level_start(p, carry):
        base = (p + 1) // 2
        side = base + 2 * ((p + 1) % 2) - 1
        spread = jnp.dot(my, halves(0.75 * xc[base] + 0.25 * xc[side], 0), preferred_element_type=F32)
        here = ((p >= 3) | has_zm) & ((p < ldepth + 3) | has_zp)
        keep = inside & here
        kappa = jnp.where(keep, lookup(lid[p], table), 0.0)
        field = jnp.where(keep, li[p] + spread, 0.0)
        lk[p] = kappa
        lv[p] = field
        lkv[p] = kappa * field
        return carry

    def level_sum(ref, p):
        field = ref[p]
        return (
            pltpu.roll(field, 1, 0) + pltpu.roll(field, wr - 1, 0)
            + pltpu.roll(field, 1, 1) + pltpu.roll(field, wc - 1, 1)
            + ref[p - 1] + ref[p + 1]
        )

    def level_one(p, carry):
        kappa = lk[p]
        inv = inverse(kappa, level_sum(lk, p))
        linv[p] = inv
        rhs = jnp.where(inv > 0.0, lr[p - 1], 0.0)
        goal = (2.0 * rhs + kappa * level_sum(lv, p) + level_sum(lkv, p)) * inv
        field = lv[p]
        new = field + (goal - field) * (1.0 / 1.2)
        lv1[p] = new
        lkv1[p] = kappa * new
        return carry

    def level_two(p, carry):
        inv = linv[p]
        rhs = jnp.where(inv > 0.0, lr[p - 1], 0.0)
        goal = (2.0 * rhs + lk[p] * level_sum(lv1, p) + level_sum(lkv1, p)) * inv
        mid[p - 2] = (3.0 / 14.0) * lv1[p] - (2.0 / 7.0) * lv[p] + (15.0 / 14.0) * goal
        return carry

    def spread_rows(p, carry):
        pm[p - 2] = jnp.dot(my2, halves(wide[p - 2], 0), preferred_element_type=F32)
        return carry

    def level_finish(low, high):
        lax.fori_loop(low, high, level_two, 0)
        part = mid[low - 2:high - 2].reshape((high - low) * wr, wc)
        wide[low - 2:high - 2] = jnp.dot(
            halves(part, 1), mx2, preferred_element_type=F32
        ).reshape(high - low, wr, cols + 128)
        lax.fori_loop(low, high, spread_rows, 0)

    lax.fori_loop(3, planes - 3, level_start, 0)
    lax.fori_loop(4, planes - 4, level_one, 0)
    level_finish(5, planes - 5)

    receive(level_in)
    for src, dst in ((fid_hbm, fidz), (fi_hbm, fiz)):
        fine_in.append(send(src.at[pl.ds(depth - 1, 1)], dst.at[pl.ds(0, 1)], zp, has_zp, has_zm))
        fine_in.append(send(src.at[pl.ds(0, 1)], dst.at[pl.ds(1, 1)], zm, has_zm, has_zp))

    lax.fori_loop(0, 3, level_start, 0)
    lax.fori_loop(planes - 3, planes, level_start, 0)
    lax.fori_loop(1, 4, level_one, 0)
    lax.fori_loop(planes - 4, planes - 1, level_one, 0)
    level_finish(2, 5)
    level_finish(planes - 5, planes - 2)

    local[6].wait()
    receive(fine_in)
    lanes = lax.broadcasted_iota(jnp.int32, (16, 128), 1)
    edge_in = jnp.where(wa == 0, 0, 64)
    edge_in = (lanes >= edge_in) & (lanes < edge_in + 64)

    def spread_at(j, where, width):
        base = (j + 1) // 2
        side = base + 2 * ((j + 1) % 2) - 1
        return 0.75 * pm[(base,) + where + (width,)] + 0.25 * pm[(side,) + where + (width,)]

    def put(j, where, width, kappa, field):
        fk[(j,) + where + (width,)] = kappa
        fv[(j,) + where + (width,)] = field
        fkv[(j,) + where + (width,)] = kappa * field

    for n, j, there in ((0, 0, has_zm), (1, depth + 1, has_zp)):
        for r in range(0, rows, 16):
            at = (pl.ds(8 + r, 16),)
            put(
                j, at, main,
                jnp.where(there, lookup(fidz[n, r:r + 16, :], table), 0.0),
                jnp.where(there, fiz[n, r:r + 16, :] + spread_at(j, at, main), 0.0),
            )

    def fine_start(j, carry):
        for r in range(0, rows, 16):
            at = (pl.ds(8 + r, 16),)
            field = fi[j - 1, r:r + 16, :] + spread_at(j, at, main)
            fv[j, 8 + r:24 + r, main] = field
            fkv[j, 8 + r:24 + r, main] = fk[j, 8 + r:24 + r, main] * field
            put(
                j, at, rim,
                jnp.where(edge_in, lookup(fidx[j - 1, r:r + 16, :], table), 0.0),
                jnp.where(edge_in, fix[j - 1, r:r + 16, :] + spread_at(j, at, rim), 0.0),
            )
        for n, row, there in ((0, 7, has_ym), (1, rows + 8, has_yp)):
            at = (pl.ds(row, 1),)
            put(
                j, at, main,
                jnp.where(there, lookup(yidrecv[n, pl.ds(j - 1, 1), :], table), 0.0),
                jnp.where(there, yrecv[n, pl.ds(j - 1, 1), :] + spread_at(j, at, main), 0.0),
            )
        return carry

    lax.fori_loop(1, depth + 1, fine_start, 0)

    def fine_sum(ref, j, r):
        centre = ref[j, r:r + 16, :]
        return (
            pltpu.roll(centre, 1, 1)[:, :cols] + pltpu.roll(centre, cols + 127, 1)[:, :cols]
            + ref[j, r - 1:r + 15, main] + ref[j, r + 1:r + 17, main]
            + ref[j - 1, r:r + 16, main] + ref[j + 1, r:r + 16, main]
        )

    def fine_one(j, carry):
        for r in range(0, rows, 16):
            s = 8 + r
            kappa = fk[j, s:s + 16, main]
            inv = 1.0 / (6.0 * kappa + fine_sum(fk, j, s))
            finv[j - 1, r:r + 16, :] = inv
            goal = (2.0 * fr[j - 1, r:r + 16, :] + kappa * fine_sum(fv, j, s) + fine_sum(fkv, j, s)) * inv
            field = fv[j, s:s + 16, main]
            new = field + (goal - field) * (1.0 / 1.2)
            fv1[j, s:s + 16, main] = new
            fkv1[j, s:s + 16, main] = kappa * new
        for n, row in ((0, rows + 7), (1, 8)):
            vysend[n, pl.ds(j - 1, 1), :] = fv1[j, pl.ds(row, 1), main]
        return carry

    own = pl.ds(8, rows)

    def rim_sends(first, count):
        group = pl.ds(first, count)
        return [
            send(fv1.at[pl.ds(first + 1, count), own, pl.ds(edge0, 128)], vx.at[group], other, None, None),
            send(vysend.at[0, group], vyrecv.at[0, group], yp, has_yp, has_ym),
            send(vysend.at[1, group], vyrecv.at[1, group], ym, has_ym, has_yp),
        ]

    half = depth // 2
    lax.fori_loop(0, 2, lambda i, carry: fine_one(1 + i * (depth - 1), carry), 0)
    faces = [
        send(fv1.at[pl.ds(depth, 1), own, pl.ds(0, cols)], fv1.at[pl.ds(0, 1), own, pl.ds(0, cols)], zp, has_zp, has_zm),
        send(fv1.at[pl.ds(1, 1), own, pl.ds(0, cols)], fv1.at[pl.ds(depth + 1, 1), own, pl.ds(0, cols)], zm, has_zm, has_zp),
    ]
    lax.fori_loop(2, half + 1, fine_one, 0)
    rims_low = rim_sends(0, half)
    lax.fori_loop(half + 1, depth, fine_one, 0)
    rims_high = rim_sends(half, depth - half)

    def fine_rims(j, carry):
        for r in range(0, rows, 16):
            s = 8 + r
            field = jnp.where(edge_in, vx[j - 1, r:r + 16, :], 0.0)
            fv1[j, s:s + 16, rim] = field
            fkv1[j, s:s + 16, rim] = fk[j, s:s + 16, rim] * field
        for n, row, there in ((0, 7, has_ym), (1, rows + 8, has_yp)):
            field = jnp.where(there, vyrecv[n, pl.ds(j - 1, 1), :], 0.0)
            fv1[j, pl.ds(row, 1), main] = field
            fkv1[j, pl.ds(row, 1), main] = fk[j, pl.ds(row, 1), main] * field
        return carry

    def fine_two(j, carry):
        fine_rims(j, 0)
        for r in range(0, rows, 16):
            s = 8 + r
            goal = (
                2.0 * fr[j - 1, r:r + 16, :] + fk[j, s:s + 16, main] * fine_sum(fv1, j, s) + fine_sum(fkv1, j, s)
            ) * finv[j - 1, r:r + 16, :]
            out_ref[j - 1, r:r + 16, :] = (
                (3.0 / 14.0) * fv1[j, s:s + 16, main] - (2.0 / 7.0) * fv[j, s:s + 16, main] + (15.0 / 14.0) * goal
            )
        return carry

    receive(rims_low)
    receive(faces)
    sent(faces)
    for j, there in ((0, has_zm), (depth + 1, has_zp)):
        for r in range(8, rows + 8, 16):
            field = jnp.where(there, fv1[j, r:r + 16, main], 0.0)
            fv1[j, r:r + 16, main] = field
            fkv1[j, r:r + 16, main] = fk[j, r:r + 16, main] * field
    lax.fori_loop(1, half + 1, fine_two, 0)
    receive(rims_high)
    lax.fori_loop(half + 1, depth + 1, fine_two, 0)
    sent(coarse_in + level_in + fine_in + rims_low + rims_high)


def per_device(sizes, *args):
    fine, level, coarse = args[0], args[3], args[6]
    count_z, count_y, wr, wc = sizes
    depth, rows, cols = fine.shape
    ldepth = level.shape[0]
    i32 = jnp.int32
    planes = ldepth + 6
    big = (depth + 2, rows + 16, cols + 128)
    small = (planes, wr, wc)

    def vmem(shape, dtype=F32):
        return pltpu.VMEM(shape, dtype)

    scratch = [
        vmem(fine.shape), vmem(fine.shape), vmem(fine.shape, i32),
        vmem((2, rows, cols)), vmem((2, rows, cols), i32),
        vmem((depth, rows, 128)), vmem((depth, rows, 128), i32),
        vmem((2, depth, cols)), vmem((2, depth, cols), i32),
        vmem((2, depth, cols)), vmem((2, depth, cols), i32),
        vmem(small), vmem((ldepth + 4, wr, wc)), vmem(small, i32),
        vmem((ldepth // 2 + 4,) + coarse.shape[1:]),
        vmem((ldepth // 2 + 4, coarse.shape[1], wc)),
        vmem(small), vmem(small), vmem(small), vmem(small), vmem(small), vmem(small),
        vmem((ldepth + 2, wr, wc)), vmem((ldepth + 2, wr, cols + 128)), vmem((ldepth + 2, rows + 16, cols + 128)),
        vmem(big), vmem(big), vmem(big), vmem(big), vmem(big), vmem(fine.shape),
        vmem((depth, rows, 128)), vmem((2, depth, cols)), vmem((2, depth, cols)),
        pltpu.SemaphoreType.DMA((7,)),
        pltpu.SemaphoreType.DMA((26,)),
        pltpu.SemaphoreType.DMA((26,)),
    ]
    return pl.pallas_call(
        functools.partial(kernel, sizes),
        out_shape=jax.ShapeDtypeStruct(fine.shape, F32),
        in_specs=[pl.BlockSpec(memory_space=pl.ANY)] * 7 + [pl.BlockSpec(memory_space=pltpu.SMEM)],
        out_specs=pl.BlockSpec(memory_space=pltpu.VMEM),
        scratch_shapes=scratch,
        compiler_params=pltpu.CompilerParams(
            collective_id=0, has_side_effects=True, vmem_limit_bytes=56 * 1024 * 1024
        ),
    )(*args)


def solution(mesh):
    count_z, count_y = mesh.shape["gx"], mesh.shape["gy"]
    sizes = (count_z, count_y, 40 if count_y <= 2 else 48, 384)
    return jax.shard_map(
        functools.partial(per_device, sizes),
        mesh=mesh,
        in_specs=(
            P(("grp", "gx"), "gy", "wa"),
            P(("grp", "gx"), "gy", "wa"),
            P(("grp", "gx"), "gy", "wa"),
            P(("grp", "gx"), None, None),
            P(("grp", "gx"), None, None),
            P(("grp", "gx"), None, None),
            P(("grp", "gx"), None, None),
            P(),
        ),
        out_specs=P(("grp", "gx"), "gy", "wa"),
        check_vma=False,
    )
```

```python
import functools

import jax
import jax.numpy as jnp
from jax import lax
from jax.experimental import pallas as pl
from jax.experimental.pallas import tpu as pltpu
from jax.sharding import PartitionSpec as P

F32 = jnp.float32
BF16 = jnp.bfloat16


def lookup(ids, table):
    kappa = jnp.zeros(ids.shape, F32)
    for material, value in enumerate(table):
        kappa = jnp.where(ids == material, value, kappa)
    return kappa


def weights_of(shape, fine_axis, first, total, offset, wrap=None):
    fine = lax.broadcasted_iota(jnp.int32, shape, fine_axis)
    if wrap is not None:
        fine = jnp.where(fine >= wrap[0], fine - wrap[1], fine)
    fine = fine + first
    base = fine >> 1
    side = base + 2 * (fine & 1) - 1
    coarse = lax.broadcasted_iota(jnp.int32, shape, 1 - fine_axis) + offset
    main = jnp.where(coarse == base, 0.75, 0.0)
    both = jnp.where(coarse == side, 0.25, main)
    return jnp.where((fine >= 0) & (fine < total), both, 0.0).astype(F32)


def halves(field, axis):
    high = field.astype(BF16).astype(F32)
    return jnp.concatenate([high, field - high], axis=axis).astype(BF16)


def twice(weights, axis):
    return jnp.concatenate([weights, weights], axis=axis).astype(BF16)


def inverse(kappa, around):
    return jnp.where(kappa > 0.0, 1.0 / (6.0 * kappa + around), 0.0)


def kernel(
    sizes,
    fi_hbm, fr_hbm, fid_hbm, li_hbm, lr_hbm, lid_hbm, co_hbm, table_ref,
    out_ref,
    fi, fr, fid, fiz, fidz, fix, fidx, ysend, yidsend, yrecv, yidrecv,
    li, lr, lid, co, xc,
    lk, lv, lkv, lv1, lkv1, linv, mid, wide, pm,
    fk, fv, fkv, fv1, fkv1, finv, vx, vysend, vyrecv,
    local_sem, send_sem, recv_sem,
):
    count_z, count_y, wr, wc = sizes
    depth, rows, cols = fi.shape
    ldepth, lrows, lcols = li_hbm.shape
    crows, ccols = co_hbm.shape[1:]
    gx = lax.axis_index("gx")
    gy = lax.axis_index("gy")
    wa = lax.axis_index("wa")
    has_zm, has_zp = gx > 0, gx < count_z - 1
    has_ym, has_yp = gy > 0, gy < count_y - 1
    row0 = pl.multiple_of(jnp.clip(gy * (rows // 2) - 8, 0, lrows - wr), 8)
    col0 = pl.multiple_of(wa * (lcols - wc), 128)
    zm, zp = {"gx": gx - 1}, {"gx": gx + 1}
    ym, yp = {"gy": gy - 1}, {"gy": gy + 1}
    other = {"wa": 1 - wa}

    barrier = pltpu.get_barrier_semaphore()
    sides = ((has_zm, zm), (has_zp, zp), (has_ym, ym), (has_yp, yp))
    for there, who in sides:
        @pl.when(there)
        def _(who=who):
            pl.semaphore_signal(barrier, 1, device_id=who, device_id_type=pl.DeviceIdType.MESH)
    pl.semaphore_signal(barrier, 1, device_id=other, device_id_type=pl.DeviceIdType.MESH)

    local = []
    for src, dst in (
        (co_hbm, co.at[pl.ds(2, ldepth // 2)]),
        (li_hbm.at[:, pl.ds(row0, wr), pl.ds(col0, wc)], li.at[pl.ds(3, ldepth)]),
        (lid_hbm.at[:, pl.ds(row0, wr), pl.ds(col0, wc)], lid.at[pl.ds(3, ldepth)]),
        (lr_hbm.at[:, pl.ds(row0, wr), pl.ds(col0, wc)], lr.at[pl.ds(2, ldepth)]),
        (fi_hbm, fi), (fid_hbm, fid), (fr_hbm, fr),
    ):
        copy = pltpu.make_async_copy(src, dst, local_sem.at[len(local)])
        copy.start()
        local.append(copy)

    present = [jnp.where(there, 1, 0) for there, _ in sides]
    pl.semaphore_wait(barrier, present[0] + present[1] + present[2] + present[3] + 1)

    used = [0]

    def send(src, dst, who, to_there, from_there):
        index = used[0]
        used[0] += 1
        copy = pltpu.make_async_remote_copy(
            src_ref=src, dst_ref=dst, send_sem=send_sem.at[index], recv_sem=recv_sem.at[index],
            device_id=who, device_id_type=pl.DeviceIdType.MESH,
        )
        if to_there is None:
            copy.start()
        else:
            pl.when(to_there)(copy.start)
        return copy, to_there, from_there

    def receive(copies):
        for copy, _, there in copies:
            if there is None:
                copy.wait_recv()
            else:
                pl.when(there)(copy.wait_recv)

    def sent(copies):
        for copy, there, _ in copies:
            if there is None:
                copy.wait_send()
            else:
                pl.when(there)(copy.wait_send)

    def z_pair(src, dst, width, own):
        count = src.shape[0]
        lanes = src.shape[2] // 2
        window = dst.shape[1] == wr
        height = pl.ds(row0, wr) if window else slice(None)
        src0 = pl.multiple_of(wa * lanes, 128)
        dst0 = pl.multiple_of(wa * (dst.shape[2] - lanes), 128)
        take, place = pl.ds(src0, lanes), pl.ds(dst0, lanes)
        return [
            send(src.at[pl.ds(count - width, width), height, take], dst.at[pl.ds(own - width, width), :, place], zp, has_zp, has_zm),
            send(src.at[pl.ds(0, width), height, take], dst.at[pl.ds(own + count, width), :, place], zm, has_zm, has_zp),
        ]

    def forward(pair, src, dst, width, own):
        window = dst.shape[1] == wr
        lanes = src.shape[2] // 2
        from0 = pl.multiple_of(jnp.where(wa == 0, lanes - 128, dst.shape[2] - lanes) if window else wa * lanes, 128)
        to0 = pl.multiple_of(wa * (dst.shape[2] - 128) if window else wa * lanes, 128)
        width_lanes = 128 if window else lanes
        result = []
        for copy, first, there in ((pair[0], own - width, has_zm), (pair[1], own + src.shape[0], has_zp)):
            receive([copy])
            layers = pl.ds(first, width)
            result.append(send(
                dst.at[layers, :, pl.ds(from0, width_lanes)], dst.at[layers, :, pl.ds(to0, width_lanes)],
                other, there, there,
            ))
        return result

    coarse_in = z_pair(co_hbm, co, 2, 2)
    level_in = z_pair(li_hbm, li, 3, 3)
    level_in += z_pair(lid_hbm, lid, 3, 3)
    level_in += z_pair(lr_hbm, lr, 2, 2)
    edge0 = pl.multiple_of((1 - wa) * (cols - 128), 128)
    fine_in = [
        send(fid_hbm.at[:, :, pl.ds(edge0, 128)], fidx, other, None, None),
        send(fi_hbm.at[:, :, pl.ds(edge0, 128)], fix, other, None, None),
    ]
    local[4].wait()
    local[5].wait()
    for src, pack, dst in ((fid, yidsend, yidrecv), (fi, ysend, yrecv)):
        for z in range(depth):
            pack[0, pl.ds(z, 1), :] = src[z, pl.ds(rows - 1, 1), :]
            pack[1, pl.ds(z, 1), :] = src[z, pl.ds(0, 1), :]
        fine_in.append(send(pack.at[0], dst.at[0], yp, has_yp, has_ym))
        fine_in.append(send(pack.at[1], dst.at[1], ym, has_ym, has_yp))

    table = [table_ref[m] for m in range(table_ref.shape[0])]
    main = slice(0, cols)
    rim = slice(cols, cols + 128)

    def fine_kappa(j, carry):
        for r in range(0, rows, 16):
            fk[j, 8 + r:24 + r, main] = lookup(fid[j - 1, r:r + 16, :], table)
        return carry

    lax.fori_loop(1, depth + 1, fine_kappa, 0)

    coarse_more = forward(coarse_in, co_hbm, co, 2, 2)
    mx = twice(weights_of((ccols, wc), 1, col0, lcols, 0), 0)
    my = twice(weights_of((wr, crows), 0, row0, lrows, 0), 1)
    mx2 = twice(weights_of((wc, cols + 128), 1, wa * cols, 2 * lcols, col0, (cols + 64, cols + 128)), 0)
    my2 = twice(weights_of((rows + 16, wr), 0, gy * rows - 8, 2 * lrows, row0), 1)

    for copy in local[:4]:
        copy.wait()
    receive(coarse_more)

    planes = ldepth + 6
    cplanes = ldepth // 2 + 4
    coarse = jnp.concatenate(
        [jnp.where(has_zm, co[0:2], 0.0), co[2:cplanes - 2], jnp.where(has_zp, co[cplanes - 2:], 0.0)], axis=0
    )
    xc[...] = jnp.dot(
        halves(coarse.reshape(cplanes * crows, ccols), 1), mx, preferred_element_type=F32
    ).reshape(cplanes, crows, wc)
    lrow = lax.broadcasted_iota(jnp.int32, (wr, wc), 0)
    lcol = lax.broadcasted_iota(jnp.int32, (wr, wc), 1)
    inside = (lrow != jnp.where(gy == 0, wr - 1, 0)) & (lcol != jnp.where(wa == 0, wc - 1, 0))

    def level_start(p, carry):
        base = (p + 1) // 2
        side = base + 2 * ((p + 1) % 2) - 1
        spread = jnp.dot(my, halves(0.75 * xc[base] + 0.25 * xc[side], 0), preferred_element_type=F32)
        here = ((p >= 3) | has_zm) & ((p < ldepth + 3) | has_zp)
        keep = inside & here
        kappa = jnp.where(keep, lookup(lid[p], table), 0.0)
        field = jnp.where(keep, li[p] + spread, 0.0)
        lk[p] = kappa
        lv[p] = field
        lkv[p] = kappa * field
        return carry

    def level_sum(ref, p):
        field = ref[p]
        return (
            pltpu.roll(field, 1, 0) + pltpu.roll(field, wr - 1, 0)
            + pltpu.roll(field, 1, 1) + pltpu.roll(field, wc - 1, 1)
            + ref[p - 1] + ref[p + 1]
        )

    def level_one(p, carry):
        kappa = lk[p]
        inv = inverse(kappa, level_sum(lk, p))
        linv[p] = inv
        rhs = jnp.where(inv > 0.0, lr[p - 1], 0.0)
        goal = (2.0 * rhs + kappa * level_sum(lv, p) + level_sum(lkv, p)) * inv
        field = lv[p]
        new = field + (goal - field) * (1.0 / 1.2)
        lv1[p] = new
        lkv1[p] = kappa * new
        return carry

    def level_two(p, carry):
        inv = linv[p]
        rhs = jnp.where(inv > 0.0, lr[p - 1], 0.0)
        goal = (2.0 * rhs + lk[p] * level_sum(lv1, p) + level_sum(lkv1, p)) * inv
        mid[p - 2] = (3.0 / 14.0) * lv1[p] - (2.0 / 7.0) * lv[p] + (15.0 / 14.0) * goal
        return carry

    def spread_rows(p, carry):
        pm[p - 2] = jnp.dot(my2, halves(wide[p - 2], 0), preferred_element_type=F32)
        return carry

    def level_finish(low, high):
        lax.fori_loop(low, high, level_two, 0)
        part = mid[low - 2:high - 2].reshape((high - low) * wr, wc)
        wide[low - 2:high - 2] = jnp.dot(
            halves(part, 1), mx2, preferred_element_type=F32
        ).reshape(high - low, wr, cols + 128)
        lax.fori_loop(low, high, spread_rows, 0)

    lax.fori_loop(3, planes - 3, level_start, 0)
    lax.fori_loop(4, planes - 4, level_one, 0)
    level_finish(5, planes - 5)

    level_more = forward(level_in[0:2], li_hbm, li, 3, 3)
    level_more += forward(level_in[2:4], lid_hbm, lid, 3, 3)
    level_more += forward(level_in[4:6], lr_hbm, lr, 2, 2)
    for src, dst in ((fid_hbm, fidz), (fi_hbm, fiz)):
        fine_in.append(send(src.at[pl.ds(depth - 1, 1)], dst.at[pl.ds(0, 1)], zp, has_zp, has_zm))
        fine_in.append(send(src.at[pl.ds(0, 1)], dst.at[pl.ds(1, 1)], zm, has_zm, has_zp))

    receive(level_more)
    lax.fori_loop(0, 3, level_start, 0)
    lax.fori_loop(planes - 3, planes, level_start, 0)
    lax.fori_loop(1, 4, level_one, 0)
    lax.fori_loop(planes - 4, planes - 1, level_one, 0)
    level_finish(2, 5)
    level_finish(planes - 5, planes - 2)

    local[6].wait()
    receive(fine_in)
    lanes = lax.broadcasted_iota(jnp.int32, (16, 128), 1)
    edge_in = jnp.where(wa == 0, 0, 64)
    edge_in = (lanes >= edge_in) & (lanes < edge_in + 64)

    def spread_at(j, where, width):
        base = (j + 1) // 2
        side = base + 2 * ((j + 1) % 2) - 1
        return 0.75 * pm[(base,) + where + (width,)] + 0.25 * pm[(side,) + where + (width,)]

    def put(j, where, width, kappa, field):
        fk[(j,) + where + (width,)] = kappa
        fv[(j,) + where + (width,)] = field
        fkv[(j,) + where + (width,)] = kappa * field

    for n, j, there in ((0, 0, has_zm), (1, depth + 1, has_zp)):
        for r in range(0, rows, 16):
            at = (pl.ds(8 + r, 16),)
            put(
                j, at, main,
                jnp.where(there, lookup(fidz[n, r:r + 16, :], table), 0.0),
                jnp.where(there, fiz[n, r:r + 16, :] + spread_at(j, at, main), 0.0),
            )

    def fine_start(j, carry):
        for r in range(0, rows, 16):
            at = (pl.ds(8 + r, 16),)
            field = fi[j - 1, r:r + 16, :] + spread_at(j, at, main)
            fv[j, 8 + r:24 + r, main] = field
            fkv[j, 8 + r:24 + r, main] = fk[j, 8 + r:24 + r, main] * field
            put(
                j, at, rim,
                jnp.where(edge_in, lookup(fidx[j - 1, r:r + 16, :], table), 0.0),
                jnp.where(edge_in, fix[j - 1, r:r + 16, :] + spread_at(j, at, rim), 0.0),
            )
        for n, row, there in ((0, 7, has_ym), (1, rows + 8, has_yp)):
            at = (pl.ds(row, 1),)
            put(
                j, at, main,
                jnp.where(there, lookup(yidrecv[n, pl.ds(j - 1, 1), :], table), 0.0),
                jnp.where(there, yrecv[n, pl.ds(j - 1, 1), :] + spread_at(j, at, main), 0.0),
            )
        return carry

    lax.fori_loop(1, depth + 1, fine_start, 0)

    def fine_sum(ref, j, r):
        centre = ref[j, r:r + 16, :]
        return (
            pltpu.roll(centre, 1, 1)[:, :cols] + pltpu.roll(centre, cols + 127, 1)[:, :cols]
            + ref[j, r - 1:r + 15, main] + ref[j, r + 1:r + 17, main]
            + ref[j - 1, r:r + 16, main] + ref[j + 1, r:r + 16, main]
        )

    def fine_one(j, carry):
        for r in range(0, rows, 16):
            s = 8 + r
            kappa = fk[j, s:s + 16, main]
            inv = 1.0 / (6.0 * kappa + fine_sum(fk, j, s))
            finv[j - 1, r:r + 16, :] = inv
            goal = (2.0 * fr[j - 1, r:r + 16, :] + kappa * fine_sum(fv, j, s) + fine_sum(fkv, j, s)) * inv
            field = fv[j, s:s + 16, main]
            new = field + (goal - field) * (1.0 / 1.2)
            fv1[j, s:s + 16, main] = new
            fkv1[j, s:s + 16, main] = kappa * new
        for n, row in ((0, rows + 7), (1, 8)):
            vysend[n, pl.ds(j - 1, 1), :] = fv1[j, pl.ds(row, 1), main]
        return carry

    own = pl.ds(8, rows)

    def rim_sends(first, count):
        group = pl.ds(first, count)
        return [
            send(fv1.at[pl.ds(first + 1, count), own, pl.ds(edge0, 128)], vx.at[group], other, None, None),
            send(vysend.at[0, group], vyrecv.at[0, group], yp, has_yp, has_ym),
            send(vysend.at[1, group], vyrecv.at[1, group], ym, has_ym, has_yp),
        ]

    half = depth // 2
    lax.fori_loop(0, 2, lambda i, carry: fine_one(1 + i * (depth - 1), carry), 0)
    faces = [
        send(fv1.at[pl.ds(depth, 1), own, pl.ds(0, cols)], fv1.at[pl.ds(0, 1), own, pl.ds(0, cols)], zp, has_zp, has_zm),
        send(fv1.at[pl.ds(1, 1), own, pl.ds(0, cols)], fv1.at[pl.ds(depth + 1, 1), own, pl.ds(0, cols)], zm, has_zm, has_zp),
    ]
    lax.fori_loop(2, half + 1, fine_one, 0)
    rims_low = rim_sends(0, half)
    lax.fori_loop(half + 1, depth, fine_one, 0)
    rims_high = rim_sends(half, depth - half)

    def fine_rims(j, carry):
        for r in range(0, rows, 16):
            s = 8 + r
            field = jnp.where(edge_in, vx[j - 1, r:r + 16, :], 0.0)
            fv1[j, s:s + 16, rim] = field
            fkv1[j, s:s + 16, rim] = fk[j, s:s + 16, rim] * field
        for n, row, there in ((0, 7, has_ym), (1, rows + 8, has_yp)):
            field = jnp.where(there, vyrecv[n, pl.ds(j - 1, 1), :], 0.0)
            fv1[j, pl.ds(row, 1), main] = field
            fkv1[j, pl.ds(row, 1), main] = fk[j, pl.ds(row, 1), main] * field
        return carry

    def fine_two(j, carry):
        fine_rims(j, 0)
        for r in range(0, rows, 16):
            s = 8 + r
            goal = (
                2.0 * fr[j - 1, r:r + 16, :] + fk[j, s:s + 16, main] * fine_sum(fv1, j, s) + fine_sum(fkv1, j, s)
            ) * finv[j - 1, r:r + 16, :]
            out_ref[j - 1, r:r + 16, :] = (
                (3.0 / 14.0) * fv1[j, s:s + 16, main] - (2.0 / 7.0) * fv[j, s:s + 16, main] + (15.0 / 14.0) * goal
            )
        return carry

    receive(rims_low)
    receive(faces)
    sent(faces)
    for j, there in ((0, has_zm), (depth + 1, has_zp)):
        for r in range(8, rows + 8, 16):
            field = jnp.where(there, fv1[j, r:r + 16, main], 0.0)
            fv1[j, r:r + 16, main] = field
            fkv1[j, r:r + 16, main] = fk[j, r:r + 16, main] * field
    lax.fori_loop(1, half + 1, fine_two, 0)
    receive(rims_high)
    lax.fori_loop(half + 1, depth + 1, fine_two, 0)
    sent(coarse_in + coarse_more + level_in + level_more + fine_in + rims_low + rims_high)


def per_device(sizes, *args):
    fine, level, coarse = args[0], args[3], args[6]
    count_z, count_y, wr, wc = sizes
    depth, rows, cols = fine.shape
    ldepth = level.shape[0]
    i32 = jnp.int32
    planes = ldepth + 6
    big = (depth + 2, rows + 16, cols + 128)
    small = (planes, wr, wc)

    def vmem(shape, dtype=F32):
        return pltpu.VMEM(shape, dtype)

    scratch = [
        vmem(fine.shape), vmem(fine.shape), vmem(fine.shape, i32),
        vmem((2, rows, cols)), vmem((2, rows, cols), i32),
        vmem((depth, rows, 128)), vmem((depth, rows, 128), i32),
        vmem((2, depth, cols)), vmem((2, depth, cols), i32),
        vmem((2, depth, cols)), vmem((2, depth, cols), i32),
        vmem(small), vmem((ldepth + 4, wr, wc)), vmem(small, i32),
        vmem((ldepth // 2 + 4,) + coarse.shape[1:]),
        vmem((ldepth // 2 + 4, coarse.shape[1], wc)),
        vmem(small), vmem(small), vmem(small), vmem(small), vmem(small), vmem(small),
        vmem((ldepth + 2, wr, wc)), vmem((ldepth + 2, wr, cols + 128)), vmem((ldepth + 2, rows + 16, cols + 128)),
        vmem(big), vmem(big), vmem(big), vmem(big), vmem(big), vmem(fine.shape),
        vmem((depth, rows, 128)), vmem((2, depth, cols)), vmem((2, depth, cols)),
        pltpu.SemaphoreType.DMA((7,)),
        pltpu.SemaphoreType.DMA((34,)),
        pltpu.SemaphoreType.DMA((34,)),
    ]
    return pl.pallas_call(
        functools.partial(kernel, sizes),
        out_shape=pltpu.VMEM(fine.shape, F32),
        in_specs=[pl.BlockSpec(memory_space=pltpu.HBM)] * 7 + [pl.BlockSpec(memory_space=pltpu.SMEM)],
        out_specs=pl.BlockSpec(memory_space=pltpu.VMEM),
        scratch_shapes=scratch,
        compiler_params=pltpu.CompilerParams(
            collective_id=0, has_side_effects=True, vmem_limit_bytes=56 * 1024 * 1024
        ),
    )(*args)


def solution(mesh):
    count_z, count_y = mesh.shape["gx"], mesh.shape["gy"]
    sizes = (count_z, count_y, 40 if count_y <= 2 else 48, 384)
    return jax.shard_map(
        functools.partial(per_device, sizes),
        mesh=mesh,
        in_specs=(
            P(("grp", "gx"), "gy", "wa"),
            P(("grp", "gx"), "gy", "wa"),
            P(("grp", "gx"), "gy", "wa"),
            P(("grp", "gx"), None, None),
            P(("grp", "gx"), None, None),
            P(("grp", "gx"), None, None),
            P(("grp", "gx"), None, None),
            P(),
        ),
        out_specs=P(("grp", "gx"), "gy", "wa"),
        check_vma=False,
    )
```

```python
import functools

import jax
import jax.numpy as jnp
from jax import lax
from jax.experimental import pallas as pl
from jax.experimental.pallas import tpu as pltpu
from jax.sharding import PartitionSpec as P

F32 = jnp.float32
BF16 = jnp.bfloat16


def lookup(ids, table):
    kappa = jnp.zeros(ids.shape, F32)
    for material, value in enumerate(table):
        kappa = jnp.where(ids == material, value, kappa)
    return kappa


def weights_of(shape, fine_axis, first, total, offset, wrap=None):
    fine = lax.broadcasted_iota(jnp.int32, shape, fine_axis)
    if wrap is not None:
        fine = jnp.where(fine >= wrap[0], fine - wrap[1], fine)
    fine = fine + first
    base = fine >> 1
    side = base + 2 * (fine & 1) - 1
    coarse = lax.broadcasted_iota(jnp.int32, shape, 1 - fine_axis) + offset
    main = jnp.where(coarse == base, 0.75, 0.0)
    both = jnp.where(coarse == side, 0.25, main)
    return jnp.where((fine >= 0) & (fine < total), both, 0.0).astype(F32)


def halves(field, axis):
    high = field.astype(BF16).astype(F32)
    return jnp.concatenate([high, field - high], axis=axis).astype(BF16)


def twice(weights, axis):
    return jnp.concatenate([weights, weights], axis=axis).astype(BF16)


def inverse(kappa, around):
    return jnp.where(kappa > 0.0, 1.0 / (6.0 * kappa + around), 0.0)


def kernel(
    sizes,
    fi_hbm, fr_hbm, fid_hbm, li_hbm, lr_hbm, lid_hbm, co_hbm, table_ref,
    out_ref,
    fi, fr, fid, fiz, fidz, fix, fidx, ysend, yidsend, yrecv, yidrecv,
    li, lr, lid, co, xc,
    lk, lv, lkv, lv1, lkv1, linv, mid, wide, pm,
    fk, fv, fkv, fv1, fkv1, finv, vx, vysend, vyrecv,
    local_sem, send_sem, recv_sem,
):
    count_z, count_y, wr, wc = sizes
    depth, rows, cols = fi.shape
    ldepth, lrows, lcols = li_hbm.shape
    crows, ccols = co_hbm.shape[1:]
    gx = lax.axis_index("gx")
    gy = lax.axis_index("gy")
    wa = lax.axis_index("wa")
    has_zm, has_zp = gx > 0, gx < count_z - 1
    has_ym, has_yp = gy > 0, gy < count_y - 1
    row0 = pl.multiple_of(jnp.clip(gy * (rows // 2) - 8, 0, lrows - wr), 8)
    col0 = pl.multiple_of(wa * (lcols - wc), 128)
    zm, zp = {"gx": gx - 1}, {"gx": gx + 1}
    ym, yp = {"gy": gy - 1}, {"gy": gy + 1}
    other = {"wa": 1 - wa}

    barrier = pltpu.get_barrier_semaphore()
    sides = ((has_zm, zm), (has_zp, zp), (has_ym, ym), (has_yp, yp))
    for there, who in sides:
        @pl.when(there)
        def _(who=who):
            pl.semaphore_signal(barrier, 1, device_id=who, device_id_type=pl.DeviceIdType.MESH)
    pl.semaphore_signal(barrier, 1, device_id=other, device_id_type=pl.DeviceIdType.MESH)

    local = []
    for src, dst in (
        (co_hbm, co.at[pl.ds(2, ldepth // 2)]),
        (li_hbm.at[:, pl.ds(row0, wr), pl.ds(col0, wc)], li.at[pl.ds(3, ldepth)]),
        (lid_hbm.at[:, pl.ds(row0, wr), pl.ds(col0, wc)], lid.at[pl.ds(3, ldepth)]),
        (lr_hbm.at[:, pl.ds(row0, wr), pl.ds(col0, wc)], lr.at[pl.ds(2, ldepth)]),
        (fi_hbm, fi), (fid_hbm, fid), (fr_hbm, fr),
    ):
        copy = pltpu.make_async_copy(src, dst, local_sem.at[len(local)])
        copy.start()
        local.append(copy)

    present = [jnp.where(there, 1, 0) for there, _ in sides]
    pl.semaphore_wait(barrier, present[0] + present[1] + present[2] + present[3] + 1)

    used = [0]

    def send(src, dst, who, to_there, from_there):
        index = used[0]
        used[0] += 1
        copy = pltpu.make_async_remote_copy(
            src_ref=src, dst_ref=dst, send_sem=send_sem.at[index], recv_sem=recv_sem.at[index],
            device_id=who, device_id_type=pl.DeviceIdType.MESH,
        )
        if to_there is None:
            copy.start()
        else:
            pl.when(to_there)(copy.start)
        return copy, to_there, from_there

    def receive(copies):
        for copy, _, there in copies:
            if there is None:
                copy.wait_recv()
            else:
                pl.when(there)(copy.wait_recv)

    def sent(copies):
        for copy, there, _ in copies:
            if there is None:
                copy.wait_send()
            else:
                pl.when(there)(copy.wait_send)

    def z_pair(src, dst, width, own):
        count = src.shape[0]
        lanes = src.shape[2] // 2
        window = dst.shape[1] == wr
        height = pl.ds(row0, wr) if window else slice(None)
        src0 = pl.multiple_of(wa * lanes, 128)
        dst0 = pl.multiple_of(wa * (dst.shape[2] - lanes), 128)
        take, place = pl.ds(src0, lanes), pl.ds(dst0, lanes)
        return [
            send(src.at[pl.ds(count - width, width), height, take], dst.at[pl.ds(own - width, width), :, place], zp, has_zp, has_zm),
            send(src.at[pl.ds(0, width), height, take], dst.at[pl.ds(own + count, width), :, place], zm, has_zm, has_zp),
        ]

    def forward(pair, src, dst, width, own):
        window = dst.shape[1] == wr
        lanes = src.shape[2] // 2
        from0 = pl.multiple_of(jnp.where(wa == 0, lanes - 128, dst.shape[2] - lanes) if window else wa * lanes, 128)
        to0 = pl.multiple_of(wa * (dst.shape[2] - 128) if window else wa * lanes, 128)
        width_lanes = 128 if window else lanes
        result = []
        for copy, first, there in ((pair[0], own - width, has_zm), (pair[1], own + src.shape[0], has_zp)):
            receive([copy])
            layers = pl.ds(first, width)
            result.append(send(
                dst.at[layers, :, pl.ds(from0, width_lanes)], dst.at[layers, :, pl.ds(to0, width_lanes)],
                other, there, there,
            ))
        return result

    coarse_in = z_pair(co_hbm, co, 2, 2)
    level_in = z_pair(li_hbm, li, 3, 3)
    level_in += z_pair(lid_hbm, lid, 3, 3)
    level_in += z_pair(lr_hbm, lr, 2, 2)
    edge0 = pl.multiple_of((1 - wa) * (cols - 128), 128)
    fine_in = [
        send(fid_hbm.at[:, :, pl.ds(edge0, 128)], fidx, other, None, None),
        send(fi_hbm.at[:, :, pl.ds(edge0, 128)], fix, other, None, None),
    ]
    local[4].wait()
    local[5].wait()
    for src, pack, dst in ((fid, yidsend, yidrecv), (fi, ysend, yrecv)):
        for z in range(depth):
            pack[0, pl.ds(z, 1), :] = src[z, pl.ds(rows - 1, 1), :]
            pack[1, pl.ds(z, 1), :] = src[z, pl.ds(0, 1), :]
        fine_in.append(send(pack.at[0], dst.at[0], yp, has_yp, has_ym))
        fine_in.append(send(pack.at[1], dst.at[1], ym, has_ym, has_yp))

    table = [table_ref[m] for m in range(table_ref.shape[0])]
    main = slice(0, cols)
    rim = slice(cols, cols + 128)

    def fine_kappa(j, carry):
        for r in range(0, rows, 16):
            fk[j, 8 + r:24 + r, main] = lookup(fid[j - 1, r:r + 16, :], table)
        return carry

    lax.fori_loop(1, depth + 1, fine_kappa, 0)

    coarse_more = forward(coarse_in, co_hbm, co, 2, 2)
    mx = twice(weights_of((ccols, wc), 1, col0, lcols, 0), 0)
    my = twice(weights_of((wr, crows), 0, row0, lrows, 0), 1)
    mx2 = twice(weights_of((wc, cols + 128), 1, wa * cols, 2 * lcols, col0, (cols + 64, cols + 128)), 0)
    my2 = twice(weights_of((rows + 16, wr), 0, gy * rows - 8, 2 * lrows, row0), 1)

    for copy in local[:4]:
        copy.wait()
    receive(coarse_more)

    planes = ldepth + 6
    cplanes = ldepth // 2 + 4
    coarse = jnp.concatenate(
        [jnp.where(has_zm, co[0:2], 0.0), co[2:cplanes - 2], jnp.where(has_zp, co[cplanes - 2:], 0.0)], axis=0
    )
    xc[...] = jnp.dot(
        halves(coarse.reshape(cplanes * crows, ccols), 1), mx, preferred_element_type=F32
    ).reshape(cplanes, crows, wc)
    lrow = lax.broadcasted_iota(jnp.int32, (wr, wc), 0)
    lcol = lax.broadcasted_iota(jnp.int32, (wr, wc), 1)
    inside = (lrow != jnp.where(gy == 0, wr - 1, 0)) & (lcol != jnp.where(wa == 0, wc - 1, 0))

    def level_start(p, carry):
        base = (p + 1) // 2
        side = base + 2 * ((p + 1) % 2) - 1
        spread = jnp.dot(my, halves(0.75 * xc[base] + 0.25 * xc[side], 0), preferred_element_type=F32)
        here = ((p >= 3) | has_zm) & ((p < ldepth + 3) | has_zp)
        keep = inside & here
        kappa = jnp.where(keep, lookup(lid[p], table), 0.0)
        field = jnp.where(keep, li[p] + spread, 0.0)
        lk[p] = kappa
        lv[p] = field
        lkv[p] = kappa * field
        return carry

    def level_sum(ref, p):
        field = ref[p]
        return (
            pltpu.roll(field, 1, 0) + pltpu.roll(field, wr - 1, 0)
            + pltpu.roll(field, 1, 1) + pltpu.roll(field, wc - 1, 1)
            + ref[p - 1] + ref[p + 1]
        )

    def level_one(p, carry):
        kappa = lk[p]
        inv = inverse(kappa, level_sum(lk, p))
        linv[p] = inv
        rhs = jnp.where(inv > 0.0, lr[p - 1], 0.0)
        goal = (2.0 * rhs + kappa * level_sum(lv, p) + level_sum(lkv, p)) * inv
        field = lv[p]
        new = field + (goal - field) * (1.0 / 1.2)
        lv1[p] = new
        lkv1[p] = kappa * new
        return carry

    def level_two(p, carry):
        inv = linv[p]
        rhs = jnp.where(inv > 0.0, lr[p - 1], 0.0)
        goal = (2.0 * rhs + lk[p] * level_sum(lv1, p) + level_sum(lkv1, p)) * inv
        mid[p - 2] = (3.0 / 14.0) * lv1[p] - (2.0 / 7.0) * lv[p] + (15.0 / 14.0) * goal
        return carry

    def spread_rows(p, carry):
        pm[p - 2] = jnp.dot(my2, halves(wide[p - 2], 0), preferred_element_type=F32)
        return carry

    def level_finish(low, high):
        lax.fori_loop(low, high, level_two, 0)
        part = mid[low - 2:high - 2].reshape((high - low) * wr, wc)
        wide[low - 2:high - 2] = jnp.dot(
            halves(part, 1), mx2, preferred_element_type=F32
        ).reshape(high - low, wr, cols + 128)
        lax.fori_loop(low, high, spread_rows, 0)

    lax.fori_loop(3, planes - 3, level_start, 0)
    lax.fori_loop(4, planes - 4, level_one, 0)
    level_finish(5, planes - 5)

    level_more = forward(level_in[0:2], li_hbm, li, 3, 3)
    level_more += forward(level_in[2:4], lid_hbm, lid, 3, 3)
    level_more += forward(level_in[4:6], lr_hbm, lr, 2, 2)
    for src, dst in ((fid_hbm, fidz), (fi_hbm, fiz)):
        fine_in.append(send(src.at[pl.ds(depth - 1, 1)], dst.at[pl.ds(0, 1)], zp, has_zp, has_zm))
        fine_in.append(send(src.at[pl.ds(0, 1)], dst.at[pl.ds(1, 1)], zm, has_zm, has_zp))

    receive(level_more)
    lax.fori_loop(0, 3, level_start, 0)
    lax.fori_loop(planes - 3, planes, level_start, 0)
    lax.fori_loop(1, 4, level_one, 0)
    lax.fori_loop(planes - 4, planes - 1, level_one, 0)
    level_finish(2, 5)
    level_finish(planes - 5, planes - 2)

    local[6].wait()
    receive(fine_in[:6])
    lanes = lax.broadcasted_iota(jnp.int32, (16, 128), 1)
    edge_in = jnp.where(wa == 0, 0, 64)
    edge_in = (lanes >= edge_in) & (lanes < edge_in + 64)

    def spread_at(j, where, width):
        base = (j + 1) // 2
        side = base + 2 * ((j + 1) % 2) - 1
        return 0.75 * pm[(base,) + where + (width,)] + 0.25 * pm[(side,) + where + (width,)]

    def put(j, where, width, kappa, field):
        fk[(j,) + where + (width,)] = kappa
        fv[(j,) + where + (width,)] = field
        fkv[(j,) + where + (width,)] = kappa * field

    def fine_start(j, carry):
        for r in range(0, rows, 16):
            at = (pl.ds(8 + r, 16),)
            field = fi[j - 1, r:r + 16, :] + spread_at(j, at, main)
            fv[j, 8 + r:24 + r, main] = field
            fkv[j, 8 + r:24 + r, main] = fk[j, 8 + r:24 + r, main] * field
            put(
                j, at, rim,
                jnp.where(edge_in, lookup(fidx[j - 1, r:r + 16, :], table), 0.0),
                jnp.where(edge_in, fix[j - 1, r:r + 16, :] + spread_at(j, at, rim), 0.0),
            )
        for n, row, there in ((0, 7, has_ym), (1, rows + 8, has_yp)):
            at = (pl.ds(row, 1),)
            put(
                j, at, main,
                jnp.where(there, lookup(yidrecv[n, pl.ds(j - 1, 1), :], table), 0.0),
                jnp.where(there, yrecv[n, pl.ds(j - 1, 1), :] + spread_at(j, at, main), 0.0),
            )
        return carry

    lax.fori_loop(1, depth + 1, fine_start, 0)

    def fine_sum(ref, j, r):
        centre = ref[j, r:r + 16, :]
        return (
            pltpu.roll(centre, 1, 1)[:, :cols] + pltpu.roll(centre, cols + 127, 1)[:, :cols]
            + ref[j, r - 1:r + 15, main] + ref[j, r + 1:r + 17, main]
            + ref[j - 1, r:r + 16, main] + ref[j + 1, r:r + 16, main]
        )

    def fine_one(j, carry):
        for r in range(0, rows, 16):
            s = 8 + r
            kappa = fk[j, s:s + 16, main]
            inv = 1.0 / (6.0 * kappa + fine_sum(fk, j, s))
            finv[j - 1, r:r + 16, :] = inv
            goal = (2.0 * fr[j - 1, r:r + 16, :] + kappa * fine_sum(fv, j, s) + fine_sum(fkv, j, s)) * inv
            field = fv[j, s:s + 16, main]
            new = field + (goal - field) * (1.0 / 1.2)
            fv1[j, s:s + 16, main] = new
            fkv1[j, s:s + 16, main] = kappa * new
        for n, row in ((0, rows + 7), (1, 8)):
            vysend[n, pl.ds(j - 1, 1), :] = fv1[j, pl.ds(row, 1), main]
        return carry

    own = pl.ds(8, rows)

    def rim_sends(first, count):
        group = pl.ds(first, count)
        return [
            send(fv1.at[pl.ds(first + 1, count), own, pl.ds(edge0, 128)], vx.at[group], other, None, None),
            send(vysend.at[0, group], vyrecv.at[0, group], yp, has_yp, has_ym),
            send(vysend.at[1, group], vyrecv.at[1, group], ym, has_ym, has_yp),
        ]

    half = depth // 2
    lax.fori_loop(2, half + 1, fine_one, 0)
    receive(fine_in[6:])
    for n, j, there in ((0, 0, has_zm), (1, depth + 1, has_zp)):
        for r in range(0, rows, 16):
            at = (pl.ds(8 + r, 16),)
            put(
                j, at, main,
                jnp.where(there, lookup(fidz[n, r:r + 16, :], table), 0.0),
                jnp.where(there, fiz[n, r:r + 16, :] + spread_at(j, at, main), 0.0),
            )

    lax.fori_loop(0, 2, lambda i, carry: fine_one(1 + i * (depth - 1), carry), 0)
    faces = [
        send(fv1.at[pl.ds(depth, 1), own, pl.ds(0, cols)], fv1.at[pl.ds(0, 1), own, pl.ds(0, cols)], zp, has_zp, has_zm),
        send(fv1.at[pl.ds(1, 1), own, pl.ds(0, cols)], fv1.at[pl.ds(depth + 1, 1), own, pl.ds(0, cols)], zm, has_zm, has_zp),
    ]
    rims_low = rim_sends(0, half)
    lax.fori_loop(half + 1, depth, fine_one, 0)
    rims_high = rim_sends(half, depth - half)

    def fine_rims(j, carry):
        for r in range(0, rows, 16):
            s = 8 + r
            field = jnp.where(edge_in, vx[j - 1, r:r + 16, :], 0.0)
            fv1[j, s:s + 16, rim] = field
            fkv1[j, s:s + 16, rim] = fk[j, s:s + 16, rim] * field
        for n, row, there in ((0, 7, has_ym), (1, rows + 8, has_yp)):
            field = jnp.where(there, vyrecv[n, pl.ds(j - 1, 1), :], 0.0)
            fv1[j, pl.ds(row, 1), main] = field
            fkv1[j, pl.ds(row, 1), main] = fk[j, pl.ds(row, 1), main] * field
        return carry

    def fine_two(j, carry):
        fine_rims(j, 0)
        for r in range(0, rows, 16):
            s = 8 + r
            goal = (
                2.0 * fr[j - 1, r:r + 16, :] + fk[j, s:s + 16, main] * fine_sum(fv1, j, s) + fine_sum(fkv1, j, s)
            ) * finv[j - 1, r:r + 16, :]
            out_ref[j - 1, r:r + 16, :] = (
                (3.0 / 14.0) * fv1[j, s:s + 16, main] - (2.0 / 7.0) * fv[j, s:s + 16, main] + (15.0 / 14.0) * goal
            )
        return carry

    receive(rims_low)
    lax.fori_loop(2, half + 1, fine_two, 0)
    receive(rims_high)
    lax.fori_loop(half + 1, depth, fine_two, 0)
    receive(faces)
    sent(faces)
    for j, there in ((0, has_zm), (depth + 1, has_zp)):
        for r in range(8, rows + 8, 16):
            field = jnp.where(there, fv1[j, r:r + 16, main], 0.0)
            fv1[j, r:r + 16, main] = field
            fkv1[j, r:r + 16, main] = fk[j, r:r + 16, main] * field
    lax.fori_loop(0, 2, lambda i, carry: fine_two(1 + i * (depth - 1), carry), 0)
    sent(coarse_in + coarse_more + level_in + level_more + fine_in + rims_low + rims_high)


def per_device(sizes, *args):
    fine, level, coarse = args[0], args[3], args[6]
    count_z, count_y, wr, wc = sizes
    depth, rows, cols = fine.shape
    ldepth = level.shape[0]
    i32 = jnp.int32
    planes = ldepth + 6
    big = (depth + 2, rows + 16, cols + 128)
    small = (planes, wr, wc)

    def vmem(shape, dtype=F32):
        return pltpu.VMEM(shape, dtype)

    scratch = [
        vmem(fine.shape), vmem(fine.shape), vmem(fine.shape, i32),
        vmem((2, rows, cols)), vmem((2, rows, cols), i32),
        vmem((depth, rows, 128)), vmem((depth, rows, 128), i32),
        vmem((2, depth, cols)), vmem((2, depth, cols), i32),
        vmem((2, depth, cols)), vmem((2, depth, cols), i32),
        vmem(small), vmem((ldepth + 4, wr, wc)), vmem(small, i32),
        vmem((ldepth // 2 + 4,) + coarse.shape[1:]),
        vmem((ldepth // 2 + 4, coarse.shape[1], wc)),
        vmem(small), vmem(small), vmem(small), vmem(small), vmem(small), vmem(small),
        vmem((ldepth + 2, wr, wc)), vmem((ldepth + 2, wr, cols + 128)), vmem((ldepth + 2, rows + 16, cols + 128)),
        vmem(big), vmem(big), vmem(big), vmem(big), vmem(big), vmem(fine.shape),
        vmem((depth, rows, 128)), vmem((2, depth, cols)), vmem((2, depth, cols)),
        pltpu.SemaphoreType.DMA((7,)),
        pltpu.SemaphoreType.DMA((34,)),
        pltpu.SemaphoreType.DMA((34,)),
    ]
    return pl.pallas_call(
        functools.partial(kernel, sizes),
        out_shape=pltpu.VMEM(fine.shape, F32),
        in_specs=[pl.BlockSpec(memory_space=pltpu.HBM)] * 7 + [pl.BlockSpec(memory_space=pltpu.SMEM)],
        out_specs=pl.BlockSpec(memory_space=pltpu.VMEM),
        scratch_shapes=scratch,
        compiler_params=pltpu.CompilerParams(
            collective_id=0, has_side_effects=True, vmem_limit_bytes=56 * 1024 * 1024
        ),
    )(*args)


def solution(mesh):
    count_z, count_y = mesh.shape["gx"], mesh.shape["gy"]
    sizes = (count_z, count_y, 40 if count_y <= 2 else 48, 384)
    return jax.shard_map(
        functools.partial(per_device, sizes),
        mesh=mesh,
        in_specs=(
            P(("grp", "gx"), "gy", "wa"),
            P(("grp", "gx"), "gy", "wa"),
            P(("grp", "gx"), "gy", "wa"),
            P(("grp", "gx"), None, None),
            P(("grp", "gx"), None, None),
            P(("grp", "gx"), None, None),
            P(("grp", "gx"), None, None),
            P(),
        ),
        out_specs=P(("grp", "gx"), "gy", "wa"),
        check_vma=False,
    )
```
